32 devices in a mesh: band: 2 (over y), inp: 4 (over z), slab: 2 (over x), pol: 2 (over core).
Axes of the slice: x: 2, y: 2, z: 4, core: 2. Of those that a mesh axis runs over, the one named last changes fastest.
Arguments:
- voltage: bfloat16 [4, 1024, 32768], P('band', ('inp', 'pol'), 'slab'), parts along dimension 0, may hold values from -8 to 7, as said below
- filter_taps: int32 [4, 512], replicated, may hold values from -128 to 127
Outputs:
- visibility: float32 [4, 64, 1024, 1024], P('band', 'slab', ('inp', 'pol')), parts along dimension 0
The draws below stay inside these ranges and needn't reach their ends.
There are 2 independent parts, one for each index of `band`. The reference program is written for one: setup_inputs(seed, part) draws one part's arguments, and reference() takes and returns one part's arrays. A program takes and returns all parts, laid end to end along the dimension named above; an argument that names none is the same for every part. Nothing has to cross between parts.
Inputs may be any that keep to these rules, and one draw needn't show every extreme that they name: `voltage`: every entry is a whole number.
All inputs are finite; a program needn't handle non-finite values.
Results may differ from the reference program's by a relative error of at most 0.0035.
Values may be sent and summed in bfloat16 or wider, within the bound.
A program may use at most 320 MiB of HBM per device.

```python
import math
import jax
import jax.numpy as jnp
from jax import lax

INPUTS = 1024
POINTS = 512
TAPS = 4
CHANNELS = 64
SPECTRA = 64


def draw_voltage(key, part):
    key = jax.random.fold_in(key, 11)
    keys = jax.random.split(key, 3)
    length = SPECTRA * POINTS
    common = jax.random.normal(keys[0], (2, 1, length), jnp.float32)
    gains = jax.random.uniform(keys[1], (1, INPUTS, 1), jnp.float32, 0.5, 1.5)
    noise = jax.random.normal(keys[2], (2, INPUTS, length), jnp.float32)
    raw = 1.5 * gains * common + 3.0 * noise
    return jnp.clip(jnp.floor(raw + 0.5), -8.0, 7.0).astype(jnp.bfloat16)


def place_ends(values, stream_key, low, high):
    place = [jax.random.randint(jax.random.fold_in(stream_key, axis), (), 0, length) for axis, length in enumerate(values.shape)]
    widest = values.shape.index(max(values.shape))
    neighbour = place[:widest] + [(place[widest] + 1) % values.shape[widest]] + place[widest + 1:]
    return values.at[tuple(place)].set(low).at[tuple(neighbour)].set(high)


def setup_inputs(seed: int = 0, part: int = 0) -> dict:
    seeds = jax.random.split(jax.random.key(seed), 3)
    part_splits = jax.random.split(jax.random.fold_in(seeds[2], part), 3)
    voltage = draw_voltage(jax.random.fold_in(jax.random.fold_in(seeds[2], part), 71), part)
    filter_taps = place_ends(jax.random.randint(seeds[1], (TAPS, POINTS), -128, 128), jax.random.fold_in(seeds[1], 1), -128, 127).astype(jnp.int32)
    return dict(voltage=voltage, filter_taps=filter_taps)


def dft_table(channel_count, points):
    channel = jnp.arange(channel_count, dtype=jnp.int32)[:, None]
    sample = jnp.arange(points, dtype=jnp.int32)[None, :]
    residue = (channel * sample) % points
    angles = residue.astype(jnp.float32) * (2.0 * math.pi / points)
    cosine = jnp.cos(angles) / 32.0
    sine_part = jnp.sin(angles) / 32.0
    real_rows = jnp.stack([cosine, sine_part], axis=1)
    imag_rows = jnp.stack([-sine_part, cosine], axis=1)
    return jnp.stack([real_rows, imag_rows], axis=0).astype(jnp.bfloat16)


def filter_bank(voltage, filter_taps, tail_rows):
    tap_count = filter_taps.shape[0]
    points = filter_taps.shape[1]
    extended = jnp.concatenate([tail_rows, voltage], axis=2).astype(jnp.float32)
    spectra_here = voltage.shape[2] // points
    frames = extended.reshape(2, voltage.shape[1], spectra_here + tap_count - 1, points)
    weights = filter_taps.astype(jnp.float32) / 128.0
    filtered = weights[0] * frames[:, :, 0:spectra_here]
    for tap_index in range(1, tap_count):
        filtered = filtered + weights[tap_index] * frames[:, :, tap_index:tap_index + spectra_here]
    return filtered.astype(jnp.bfloat16)


def reference(voltage, filter_taps):
    block_size = math.gcd(INPUTS, 32)
    block_count = INPUTS // block_size
    transform = dft_table(CHANNELS, POINTS)
    grouped = voltage.reshape(2, block_count, block_size, SPECTRA * POINTS).transpose(1, 0, 2, 3)

    def channelise(input_block):
        zeros_head = jnp.zeros((2, block_size, (TAPS - 1) * POINTS), input_block.dtype)
        filtered = filter_bank(input_block, filter_taps, zeros_head)
        return jnp.einsum("afbp,bisp->fais", transform.astype(jnp.float32), filtered.astype(jnp.float32)).astype(jnp.bfloat16)

    spectra = lax.map(channelise, grouped)
    spectra = spectra.transpose(1, 2, 0, 3, 4).reshape(CHANNELS, 2, INPUTS, SPECTRA)

    def correlate(channel_spectra):
        stacked = channel_spectra.reshape(2 * INPUTS, SPECTRA)
        products = jnp.dot(stacked, stacked.T, preferred_element_type=jnp.float32)
        real_part = products[:INPUTS, :INPUTS] + products[INPUTS:, INPUTS:]
        imag_part = products[INPUTS:, :INPUTS] - products[:INPUTS, INPUTS:]
        return real_part / (32.0 * SPECTRA), imag_part / (32.0 * SPECTRA)

    real_part, imag_part = lax.map(correlate, spectra)
    return jnp.stack([real_part, imag_part], axis=0)
```

```python
import functools
import math

import jax
import jax.numpy as jnp
import numpy as np
from jax import lax
from jax.experimental import pallas as pl
from jax.experimental.pallas import tpu as pltpu
from jax.sharding import PartitionSpec as P

CHANNELS = 64
GROUP = 8
LANES = 128
MESH = pl.DeviceIdType.MESH


def passed_along(value, axis, steps):
    count = lax.axis_size(axis)
    first, last = (max(0, -steps), min(count, count - steps))
    return lax.ppermute(value, axis, [(source, source + steps) for source in range(first, last)])


def dft_table(channel_count, points):
    channel = jnp.arange(channel_count, dtype=jnp.int32)[:, None]
    sample = jnp.arange(points, dtype=jnp.int32)[None, :]
    residue = channel * sample % points
    angles = residue.astype(jnp.float32) * (2.0 * math.pi / points)
    cosine = jnp.cos(angles) / 32.0
    sine_part = jnp.sin(angles) / 32.0
    real_rows = jnp.stack([cosine, sine_part], axis=1)
    imag_rows = jnp.stack([-sine_part, cosine], axis=1)
    return jnp.stack([real_rows, imag_rows], axis=0).astype(jnp.bfloat16)


def filter_bank(voltage, filter_taps, tail_rows):
    tap_count = filter_taps.shape[0]
    points = filter_taps.shape[1]
    extended = jnp.concatenate([tail_rows, voltage], axis=2).astype(jnp.float32)
    spectra_here = voltage.shape[2] // points
    frames = extended.reshape(2, voltage.shape[1], spectra_here + tap_count - 1, points)
    weights = filter_taps.astype(jnp.float32) / 128.0
    filtered = weights[0] * frames[:, :, 0:spectra_here]
    for tap_index in range(1, tap_count):
        filtered = (
            filtered + weights[tap_index] * frames[:, :, tap_index : tap_index + spectra_here]
        )
    return filtered.astype(jnp.bfloat16)


def general_body(voltage, filter_taps):
    points = filter_taps.shape[1]
    tail_length = (filter_taps.shape[0] - 1) * points
    tail_rows = passed_along(voltage[:, :, voltage.shape[2] - tail_length :], "slab", 1)
    filtered = filter_bank(voltage, filter_taps, tail_rows)
    spectra = jnp.einsum(
        "afbp,bisp->fais", dft_table(CHANNELS, points), filtered, preferred_element_type=jnp.float32
    ).astype(jnp.bfloat16)
    turned = lax.all_to_all(spectra, "slab", split_axis=0, concat_axis=3, tiled=True)
    row_count = turned.shape[2]
    left = turned.reshape(turned.shape[0], 2 * row_count, turned.shape[3])
    incoming = lax.all_gather(turned, ("inp", "pol"), axis=2, tiled=True)
    col_count = incoming.shape[2]
    right = incoming.reshape(incoming.shape[0], 2 * col_count, incoming.shape[3])
    products = jnp.einsum("fis,fjs->fij", left, right, preferred_element_type=jnp.float32)
    real_part = products[:, :row_count, :col_count] + products[:, row_count:, col_count:]
    imag_part = products[:, row_count:, :col_count] - products[:, :row_count, col_count:]
    return jnp.stack([real_part, imag_part], axis=0) / (32.0 * turned.shape[3])


def spectra_kernel(
    depth, chunks, taps_ref, table_ref, volt_ref, g_ref,
    ext, filt, ybuf, tbuf, stage, load_sem, tail_sem, local_sem, x_sem, send_sem, recv_sem,
):
    tap_count, points = taps_ref.shape
    tail = (tap_count - 1) * points
    span = GROUP * points
    half = CHANNELS // 2
    inputs = volt_ref.shape[1]
    z = lax.axis_index("inp")
    x = lax.axis_index("slab")
    c = lax.axis_index("pol")
    me = z * 2 + c
    last = chunks - 1

    barrier = pltpu.get_barrier_semaphore()
    pl.semaphore_signal(barrier, inc=1, device_id={"pol": 1 - c}, device_id_type=MESH)
    pl.semaphore_signal(barrier, inc=1, device_id={"slab": 1 - x}, device_id_type=MESH)

    @pl.when(z > 0)
    def _():
        pl.semaphore_signal(barrier, inc=1, device_id={"inp": z - 1}, device_id_type=MESH)

    @pl.when(z < depth - 1)
    def _():
        pl.semaphore_signal(barrier, inc=1, device_id={"inp": z + 1}, device_id_type=MESH)

    below = jnp.where(z > 0, 1, 0)
    above = jnp.where(z < depth - 1, 1, 0)
    peers = 2 + below + above

    def chunk_of(m):
        return m + x * (last - 2 * m)

    def load(n):
        at = pl.multiple_of(chunk_of(n) * span, span)
        return pltpu.make_async_copy(
            volt_ref.at[:, :, pl.ds(at, span)],
            ext.at[:, :, pl.ds(pl.multiple_of(at + tail, points), span)],
            load_sem.at[n],
        )

    for n in range(chunks):
        load(n).start()

    @pl.when(x == 0)
    def _():
        ext[:, :, 0:tail] = jnp.zeros((2, inputs, tail), ext.dtype)

    def tail_copy():
        return pltpu.make_async_remote_copy(
            src_ref=volt_ref.at[:, :, pl.ds(chunks * span - tail, tail)],
            dst_ref=ext.at[:, :, pl.ds(0, tail)],
            send_sem=tail_sem.at[0],
            recv_sem=tail_sem.at[1],
            device_id={"slab": 1 - x},
            device_id_type=MESH,
        )

    def compute(m):
        base = pl.multiple_of(chunk_of(m) * span, span)
        wide = 256

        for b in range(2):
            for w in range(points // wide):
                scale = [
                    taps_ref[k : k + 1, w * wide : (w + 1) * wide].astype(jnp.float32)
                    * (1.0 / 128.0)
                    for k in range(tap_count)
                ]

                def rows(r, carry):
                    row = pl.multiple_of(r * 16, 16)
                    frames = []
                    for s in range(GROUP + tap_count - 1):
                        at = pl.multiple_of(base + s * points + w * wide, wide)
                        frames.append(
                            ext[b, pl.ds(row, 16), pl.ds(at, wide)].astype(jnp.float32)
                        )
                        if s >= tap_count - 1:
                            first = s - tap_count + 1
                            total = scale[0] * frames[first]
                            for k in range(1, tap_count):
                                total = total + scale[k] * frames[first + k]
                            filt[
                                pl.ds(pl.multiple_of(first * inputs + row, 16), 16),
                                pl.ds(b * points + w * wide, wide),
                            ] = total.astype(jnp.bfloat16)
                    return carry

                lax.fori_loop(0, inputs // 16, rows, 0)
        ybuf[...] = jnp.dot(filt[...], table_ref[...], preferred_element_type=jnp.float32)
        for s in range(GROUP):
            tbuf[s * 2 * CHANNELS : (s + 1) * 2 * CHANNELS, :] = ybuf[
                s * inputs : (s + 1) * inputs, :
            ].T
        for f in range(CHANNELS):
            real = tbuf[pl.ds(f, GROUP, stride=2 * CHANNELS), :]
            imag = tbuf[pl.ds(CHANNELS + f, GROUP, stride=2 * CHANNELS), :]
            stage[m, f] = jnp.concatenate([real, imag], axis=0).astype(jnp.bfloat16)

    def remote(src, q, dev, sem, where):
        return pltpu.make_async_remote_copy(
            src_ref=src,
            dst_ref=g_ref.at[q, dev],
            send_sem=sem,
            recv_sem=recv_sem.at[q, dev],
            device_id=where,
            device_id_type=MESH,
        )

    def up(src, q, zs):
        return remote(src, q, zs * 2 + c, send_sem.at[0, q, zs], {"inp": z + 1})

    def down(src, q, zs):
        return remote(src, q, zs * 2 + c, send_sem.at[1, q, zs], {"inp": z - 1})

    def across(src, q, zs):
        return remote(src, q, zs * 2 + c, send_sem.at[2, q, zs], {"pol": 1 - c})

    def spread(src, q):
        @pl.when(z < depth - 1)
        def _():
            up(src, q, z).start()

        @pl.when(z > 0)
        def _():
            down(src, q, z).start()

        across(src, q, z).start()

    def mine(m):
        return stage.at[m, pl.ds(pl.multiple_of(x * half, half), half)]

    def theirs(m):
        return stage.at[m, pl.ds(pl.multiple_of((1 - x) * half, half), half)]

    def keep(m):
        return pltpu.make_async_copy(mine(m), g_ref.at[x * chunks + m, me], local_sem.at[m])

    def give(m):
        return remote(theirs(m), x * chunks + m, me, x_sem.at[m], {"slab": 1 - x})

    def send_own(m):
        give(m).start()
        spread(mine(m), x * chunks + m)
        keep(m).start()

    def send_given(m):
        q = (1 - x) * chunks + m
        slot = g_ref.at[q, me]
        remote(slot, q, me, x_sem.at[m], {"slab": 1 - x}).wait_recv()
        spread(slot, q)

    def forward(q, distance):
        @pl.when(z - distance >= 0)
        def _():
            zs = z - distance
            slot = g_ref.at[q, zs * 2 + c]
            up(slot, q, zs).wait_recv()

            @pl.when(z < depth - 1)
            def _():
                up(slot, q, zs).start()

            across(slot, q, zs).start()

        @pl.when(z + distance < depth)
        def _():
            zs = z + distance
            slot = g_ref.at[q, zs * 2 + c]
            down(slot, q, zs).wait_recv()

            @pl.when(z > 0)
            def _():
                down(slot, q, zs).start()

            across(slot, q, zs).start()

    load(0).wait()

    def early(m, carry):
        load(m + 1).wait()
        compute(m)

        @pl.when(m == 0)
        def _():
            pl.semaphore_wait(barrier, peers)

        send_own(m)
        return carry

    lax.fori_loop(0, last, early, 0)

    @pl.when(x == 0)
    def _():
        tail_copy().start()

    for m in range(last):
        send_given(m)

    def forward_early(distance):
        def step(m, carry):
            forward(m, distance)
            forward(chunks + m, distance)
            return carry

        lax.fori_loop(0, last, step, 0)

    for distance in range(1, depth - 1):
        forward_early(distance)

    @pl.when(x == 1)
    def _():
        tail_copy().wait_recv()

    compute(last)
    send_own(last)
    send_given(last)
    for distance in range(1, depth - 1):
        forward(last, distance)
        forward(chunks + last, distance)
    forward_early(depth - 1)
    forward(last, depth - 1)
    forward(chunks + last, depth - 1)

    def finish(q, carry):
        for zs in range(depth):
            other = zs * 2 + 1 - c
            remote(
                g_ref.at[q, other], q, other, send_sem.at[2, q, zs], {"pol": 1 - c}
            ).wait_recv()
            slot = g_ref.at[q, zs * 2 + c]

            @pl.when((z >= zs) & (z < depth - 1))
            def _():
                up(slot, q, zs).wait_send()

            @pl.when((z <= zs) & (z > 0))
            def _():
                down(slot, q, zs).wait_send()

            across(slot, q, zs).wait_send()
        return carry

    lax.fori_loop(0, 2 * chunks, finish, 0)
    for m in range(chunks):
        keep(m).wait()
        give(m).wait_send()

    @pl.when(x == 0)
    def _():
        tail_copy().wait_send()


def correlate_kernel(spectra_total, g_ref, out_ref):
    slots, devices, channels, rows, lanes = g_ref.shape
    me = lax.axis_index("inp") * 2 + lax.axis_index("pol")
    scale = 1.0 / (32.0 * spectra_total)
    for f in range(channels):
        own = g_ref[:, me, f].astype(jnp.float32) * scale
        real, imag = own[:, : rows // 2], own[:, rows // 2 :]
        straight = own.reshape(slots * rows, lanes).T
        crossed = jnp.concatenate([imag, -real], axis=1).reshape(slots * rows, lanes).T
        left = jnp.concatenate([straight, crossed], axis=0).astype(jnp.bfloat16)
        right = jnp.concatenate(
            [g_ref[:, j, f].reshape(slots * rows, lanes) for j in range(devices)], axis=1
        )
        product = jnp.dot(left, right, preferred_element_type=jnp.float32)
        out_ref[0, f] = product[:lanes]
        out_ref[1, f] = product[lanes:]


def fast_body(voltage, filter_taps):
    depth = lax.axis_size("inp")
    tap_count, points = filter_taps.shape
    inputs, samples = voltage.shape[1:]
    chunks = samples // points // GROUP
    half = CHANNELS // 2
    devices = depth * 2
    channel = np.arange(CHANNELS, dtype=np.int64)[:, None]
    angles = (channel * np.arange(points)[None, :] % points).astype(np.float32)
    angles = (angles * np.float32(2.0 * math.pi / points)).astype(np.float64)
    cosine, sine = np.cos(angles) / 32.0, np.sin(angles) / 32.0
    rows = np.concatenate(
        [np.concatenate([cosine, sine], 1), np.concatenate([-sine, cosine], 1)], 0
    )
    table = jnp.asarray(rows.T.astype(np.float32)).astype(jnp.bfloat16)
    vmem = pl.BlockSpec(memory_space=pltpu.VMEM)
    hbm = pl.BlockSpec(memory_space=pl.ANY)
    gathered = pl.pallas_call(
        functools.partial(spectra_kernel, depth, chunks),
        out_shape=jax.ShapeDtypeStruct(
            (2 * chunks, devices, half, 2 * GROUP, LANES), jnp.bfloat16
        ),
        in_specs=[vmem, vmem, hbm],
        out_specs=hbm,
        scratch_shapes=[
            pltpu.VMEM((2, inputs, samples + (tap_count - 1) * points), jnp.bfloat16),
            pltpu.VMEM((GROUP * inputs, 2 * points), jnp.bfloat16),
            pltpu.VMEM((GROUP * inputs, 2 * CHANNELS), jnp.float32),
            pltpu.VMEM((GROUP * 2 * CHANNELS, inputs), jnp.float32),
            pltpu.VMEM((chunks, CHANNELS, 2 * GROUP, inputs), jnp.bfloat16),
            pltpu.SemaphoreType.DMA((chunks,)),
            pltpu.SemaphoreType.DMA((2,)),
            pltpu.SemaphoreType.DMA((chunks,)),
            pltpu.SemaphoreType.DMA((chunks,)),
            pltpu.SemaphoreType.DMA((3, 2 * chunks, depth)),
            pltpu.SemaphoreType.DMA((2 * chunks, devices)),
        ],
        compiler_params=pltpu.CompilerParams(
            collective_id=0, has_side_effects=True, vmem_limit_bytes=40 * 1024 * 1024
        ),
        name="spectra",
    )(filter_taps, table, voltage)
    step = 2
    return pl.pallas_call(
        functools.partial(correlate_kernel, 2 * chunks * GROUP),
        grid=(half // step,),
        out_shape=jax.ShapeDtypeStruct((2, half, inputs, devices * inputs), jnp.float32),
        in_specs=[
            pl.BlockSpec(
                (2 * chunks, devices, step, 2 * GROUP, LANES), lambda f: (0, 0, f, 0, 0)
            )
        ],
        out_specs=pl.BlockSpec((2, step, inputs, devices * inputs), lambda f: (0, f, 0, 0)),
        compiler_params=pltpu.CompilerParams(vmem_limit_bytes=32 * 1024 * 1024),
        name="correlate",
    )(gathered)


def body(voltage, filter_taps):
    spectra_here = voltage.shape[2] // filter_taps.shape[1]
    suits = (
        lax.axis_size("slab") == 2
        and lax.axis_size("pol") == 2
        and voltage.shape[1] == LANES
        and filter_taps.shape[1] % 256 == 0
        and spectra_here % GROUP == 0
        and spectra_here >= 2 * GROUP
        and 1 < filter_taps.shape[0] <= GROUP + 1
    )
    return fast_body(voltage, filter_taps) if suits else general_body(voltage, filter_taps)


def solution(mesh):
    placed = (P("band", ("inp", "pol"), "slab"), P())
    return jax.shard_map(
        body,
        mesh=mesh,
        in_specs=placed,
        out_specs=P("band", "slab", ("inp", "pol"), None),
        check_vma=False,
    )
```

```python
import functools
import math

import jax
import jax.numpy as jnp
import numpy as np
from jax import lax
from jax.experimental import pallas as pl
from jax.experimental.pallas import tpu as pltpu
from jax.sharding import PartitionSpec as P

CHANNELS = 64
GROUP = 8
LANES = 128
MESH = pl.DeviceIdType.MESH


def passed_along(value, axis, steps):
    count = lax.axis_size(axis)
    first, last = (max(0, -steps), min(count, count - steps))
    return lax.ppermute(value, axis, [(source, source + steps) for source in range(first, last)])


def dft_table(channel_count, points):
    channel = jnp.arange(channel_count, dtype=jnp.int32)[:, None]
    sample = jnp.arange(points, dtype=jnp.int32)[None, :]
    residue = channel * sample % points
    angles = residue.astype(jnp.float32) * (2.0 * math.pi / points)
    cosine = jnp.cos(angles) / 32.0
    sine_part = jnp.sin(angles) / 32.0
    real_rows = jnp.stack([cosine, sine_part], axis=1)
    imag_rows = jnp.stack([-sine_part, cosine], axis=1)
    return jnp.stack([real_rows, imag_rows], axis=0).astype(jnp.bfloat16)


def filter_bank(voltage, filter_taps, tail_rows):
    tap_count = filter_taps.shape[0]
    points = filter_taps.shape[1]
    extended = jnp.concatenate([tail_rows, voltage], axis=2).astype(jnp.float32)
    spectra_here = voltage.shape[2] // points
    frames = extended.reshape(2, voltage.shape[1], spectra_here + tap_count - 1, points)
    weights = filter_taps.astype(jnp.float32) / 128.0
    filtered = weights[0] * frames[:, :, 0:spectra_here]
    for tap_index in range(1, tap_count):
        filtered = (
            filtered + weights[tap_index] * frames[:, :, tap_index : tap_index + spectra_here]
        )
    return filtered.astype(jnp.bfloat16)


def general_body(voltage, filter_taps):
    points = filter_taps.shape[1]
    tail_length = (filter_taps.shape[0] - 1) * points
    tail_rows = passed_along(voltage[:, :, voltage.shape[2] - tail_length :], "slab", 1)
    filtered = filter_bank(voltage, filter_taps, tail_rows)
    spectra = jnp.einsum(
        "afbp,bisp->fais", dft_table(CHANNELS, points), filtered, preferred_element_type=jnp.float32
    ).astype(jnp.bfloat16)
    turned = lax.all_to_all(spectra, "slab", split_axis=0, concat_axis=3, tiled=True)
    row_count = turned.shape[2]
    left = turned.reshape(turned.shape[0], 2 * row_count, turned.shape[3])
    incoming = lax.all_gather(turned, ("inp", "pol"), axis=2, tiled=True)
    col_count = incoming.shape[2]
    right = incoming.reshape(incoming.shape[0], 2 * col_count, incoming.shape[3])
    products = jnp.einsum("fis,fjs->fij", left, right, preferred_element_type=jnp.float32)
    real_part = products[:, :row_count, :col_count] + products[:, row_count:, col_count:]
    imag_part = products[:, row_count:, :col_count] - products[:, :row_count, col_count:]
    return jnp.stack([real_part, imag_part], axis=0) / (32.0 * turned.shape[3])


def spectra_kernel(
    depth, chunks, taps_hbm, table_hbm, volt_ref, g_ref,
    taps_ref, table_ref, ext, filt, ybuf, tbuf, stage, aux_sem, load_sem, tail_sem, local_sem, x_sem, send_sem, recv_sem,
):
    tap_count, points = taps_ref.shape
    tail = (tap_count - 1) * points
    span = GROUP * points
    half = CHANNELS // 2
    inputs = volt_ref.shape[1]
    z = lax.axis_index("inp")
    x = lax.axis_index("slab")
    c = lax.axis_index("pol")
    me = z * 2 + c
    last = chunks - 1

    barrier = pltpu.get_barrier_semaphore()
    pl.semaphore_signal(barrier, inc=1, device_id={"pol": 1 - c}, device_id_type=MESH)
    pl.semaphore_signal(barrier, inc=1, device_id={"slab": 1 - x}, device_id_type=MESH)

    @pl.when(z > 0)
    def _():
        pl.semaphore_signal(barrier, inc=1, device_id={"inp": z - 1}, device_id_type=MESH)

    @pl.when(z < depth - 1)
    def _():
        pl.semaphore_signal(barrier, inc=1, device_id={"inp": z + 1}, device_id_type=MESH)

    below = jnp.where(z > 0, 1, 0)
    above = jnp.where(z < depth - 1, 1, 0)
    peers = 2 + below + above

    def chunk_of(m):
        return m + x * (last - 2 * m)

    total_span = chunks * span

    def load(n):
        low = n * span + (tail if n else 0)
        size = min(span + (0 if n else tail), total_span - low)
        at = pl.multiple_of(low + x * (total_span - size - 2 * low), points)
        return pltpu.make_async_copy(
            volt_ref.at[:, :, pl.ds(at, size)],
            ext.at[:, :, pl.ds(pl.multiple_of(at + tail, points), size)],
            load_sem.at[n],
        )

    taps_copy = pltpu.make_async_copy(taps_hbm, taps_ref, aux_sem.at[0])
    table_copy = pltpu.make_async_copy(table_hbm, table_ref, aux_sem.at[1])
    load(0).start()
    taps_copy.start()
    table_copy.start()

    @pl.when(x == 0)
    def _():
        ext[:, :, 0:tail] = jnp.zeros((2, inputs, tail), ext.dtype)

    def tail_copy():
        return pltpu.make_async_remote_copy(
            src_ref=volt_ref.at[:, :, pl.ds(chunks * span - tail, tail)],
            dst_ref=ext.at[:, :, pl.ds(0, tail)],
            send_sem=tail_sem.at[0],
            recv_sem=tail_sem.at[1],
            device_id={"slab": 1 - x},
            device_id_type=MESH,
        )

    def compute(m):
        base = pl.multiple_of(chunk_of(m) * span, span)
        wide = 256

        for b in range(2):
            for w in range(points // wide):
                scale = [
                    taps_ref[k : k + 1, w * wide : (w + 1) * wide].astype(jnp.float32)
                    * (1.0 / 128.0)
                    for k in range(tap_count)
                ]

                def rows(r, carry):
                    row = pl.multiple_of(r * 16, 16)
                    frames = []
                    for s in range(GROUP + tap_count - 1):
                        at = pl.multiple_of(base + s * points + w * wide, wide)
                        frames.append(
                            ext[b, pl.ds(row, 16), pl.ds(at, wide)].astype(jnp.float32)
                        )
                        if s >= tap_count - 1:
                            first = s - tap_count + 1
                            total = scale[0] * frames[first]
                            for k in range(1, tap_count):
                                total = total + scale[k] * frames[first + k]
                            filt[
                                pl.ds(pl.multiple_of(first * inputs + row, 16), 16),
                                pl.ds(b * points + w * wide, wide),
                            ] = total.astype(jnp.bfloat16)
                    return carry

                lax.fori_loop(0, inputs // 16, rows, 0)
        ybuf[...] = jnp.dot(filt[...], table_ref[...], preferred_element_type=jnp.float32)
        for s in range(GROUP):
            tbuf[s * 2 * CHANNELS : (s + 1) * 2 * CHANNELS, :] = ybuf[
                s * inputs : (s + 1) * inputs, :
            ].T
        for f in range(CHANNELS):
            real = tbuf[pl.ds(f, GROUP, stride=2 * CHANNELS), :]
            imag = tbuf[pl.ds(CHANNELS + f, GROUP, stride=2 * CHANNELS), :]
            stage[m, f] = jnp.concatenate([real, imag], axis=0).astype(jnp.bfloat16)

    def remote(src, q, dev, sem, where):
        return pltpu.make_async_remote_copy(
            src_ref=src,
            dst_ref=g_ref.at[q, dev],
            send_sem=sem,
            recv_sem=recv_sem.at[q, dev],
            device_id=where,
            device_id_type=MESH,
        )

    def up(src, q, zs):
        return remote(src, q, zs * 2 + c, send_sem.at[0, q, zs], {"inp": z + 1})

    def down(src, q, zs):
        return remote(src, q, zs * 2 + c, send_sem.at[1, q, zs], {"inp": z - 1})

    def across(src, q, zs):
        return remote(src, q, zs * 2 + c, send_sem.at[2, q, zs], {"pol": 1 - c})

    def spread(src, q):
        @pl.when(z < depth - 1)
        def _():
            up(src, q, z).start()

        @pl.when(z > 0)
        def _():
            down(src, q, z).start()

        across(src, q, z).start()

    def mine(m):
        return stage.at[m, pl.ds(pl.multiple_of(x * half, half), half)]

    def theirs(m):
        return stage.at[m, pl.ds(pl.multiple_of((1 - x) * half, half), half)]

    def keep(m):
        return pltpu.make_async_copy(mine(m), g_ref.at[x * chunks + m, me], local_sem.at[m])

    def give(m):
        return remote(theirs(m), x * chunks + m, me, x_sem.at[m], {"slab": 1 - x})

    def send_own(m):
        give(m).start()
        spread(mine(m), x * chunks + m)
        keep(m).start()

    def send_given(m):
        q = (1 - x) * chunks + m
        slot = g_ref.at[q, me]
        remote(slot, q, me, x_sem.at[m], {"slab": 1 - x}).wait_recv()
        spread(slot, q)

    def forward(q, distance):
        @pl.when(z - distance >= 0)
        def _():
            zs = z - distance
            slot = g_ref.at[q, zs * 2 + c]
            up(slot, q, zs).wait_recv()

            @pl.when(z < depth - 1)
            def _():
                up(slot, q, zs).start()

            across(slot, q, zs).start()

        @pl.when(z + distance < depth)
        def _():
            zs = z + distance
            slot = g_ref.at[q, zs * 2 + c]
            down(slot, q, zs).wait_recv()

            @pl.when(z > 0)
            def _():
                down(slot, q, zs).start()

            across(slot, q, zs).start()

    load(0).wait()
    for n in range(1, chunks):
        load(n).start()
    taps_copy.wait()
    table_copy.wait()

    def early(m, carry):
        compute(m)

        @pl.when(m == 0)
        def _():
            pl.semaphore_wait(barrier, peers)

        send_own(m)
        for n in range(1, chunks):

            @pl.when(m == n - 1)
            def _():
                load(n).wait()

        return carry

    lax.fori_loop(0, last, early, 0)

    @pl.when(x == 0)
    def _():
        tail_copy().start()

    for m in range(last):
        send_given(m)

    def forward_early(distance):
        def step(m, carry):
            forward(m, distance)
            forward(chunks + m, distance)
            return carry

        lax.fori_loop(0, last, step, 0)

    for distance in range(1, depth - 1):
        forward_early(distance)

    @pl.when(x == 1)
    def _():
        tail_copy().wait_recv()

    compute(last)
    send_own(last)
    send_given(last)
    for distance in range(1, depth - 1):
        forward(last, distance)
        forward(chunks + last, distance)
    def finish(q, zs):
        other = zs * 2 + 1 - c
        remote(
            g_ref.at[q, other], q, other, send_sem.at[2, q, zs], {"pol": 1 - c}
        ).wait_recv()
        slot = g_ref.at[q, zs * 2 + c]

        @pl.when((z >= zs) & (z < depth - 1))
        def _():
            up(slot, q, zs).wait_send()

        @pl.when((z <= zs) & (z > 0))
        def _():
            down(slot, q, zs).wait_send()

        across(slot, q, zs).wait_send()

    def far(zs):
        return (z - zs == depth - 1) | (zs - z == depth - 1)

    def finish_near(q, carry):
        for zs in range(depth):

            @pl.when(jnp.logical_not(far(zs)))
            def _():
                finish(q, zs)

        return carry

    def finish_far(q, carry):
        for zs in (0, depth - 1):

            @pl.when(far(zs))
            def _():
                finish(q, zs)

        return carry

    lax.fori_loop(0, 2 * chunks, finish_near, 0)
    for m in range(chunks):
        keep(m).wait()
        give(m).wait_send()

    @pl.when(x == 0)
    def _():
        tail_copy().wait_send()

    forward_early(depth - 1)
    forward(last, depth - 1)
    forward(chunks + last, depth - 1)
    lax.fori_loop(0, 2 * chunks, finish_far, 0)


def correlate_kernel(spectra_total, g_ref, out_ref, buf, sem):
    slots, devices, channels, rows, lanes = g_ref.shape
    depth = buf.shape[0]
    me = lax.axis_index("inp") * 2 + lax.axis_index("pol")
    scale = 1.0 / (32.0 * spectra_total)

    def put(f, slot):
        return pltpu.make_async_copy(buf.at[slot], out_ref.at[:, f], sem.at[slot])

    def step(f, carry):
        slot = lax.rem(f, depth)

        @pl.when(f >= depth)
        def _():
            put(f - depth, slot).wait()

        own = g_ref[:, me, f].astype(jnp.float32) * scale
        real, imag = own[:, : rows // 2], own[:, rows // 2 :]
        straight = own.reshape(slots * rows, lanes).T
        crossed = jnp.concatenate([imag, -real], axis=1).reshape(slots * rows, lanes).T
        left = jnp.concatenate([straight, crossed], axis=0).astype(jnp.bfloat16)
        right = jnp.concatenate(
            [g_ref[:, j, f].reshape(slots * rows, lanes) for j in range(devices)], axis=1
        )
        product = jnp.dot(left, right, preferred_element_type=jnp.float32)
        buf[slot, 0] = product[:lanes]
        buf[slot, 1] = product[lanes:]
        put(f, slot).start()
        return carry

    lax.fori_loop(0, channels, step, 0)
    for f in range(channels - depth, channels):
        put(f, f % depth).wait()


def fast_body(voltage, filter_taps):
    depth = lax.axis_size("inp")
    tap_count, points = filter_taps.shape
    inputs, samples = voltage.shape[1:]
    chunks = samples // points // GROUP
    half = CHANNELS // 2
    devices = depth * 2
    channel = np.arange(CHANNELS, dtype=np.int64)[:, None]
    angles = (channel * np.arange(points)[None, :] % points).astype(np.float32)
    angles = (angles * np.float32(2.0 * math.pi / points)).astype(np.float64)
    cosine, sine = np.cos(angles) / 32.0, np.sin(angles) / 32.0
    rows = np.concatenate(
        [np.concatenate([cosine, sine], 1), np.concatenate([-sine, cosine], 1)], 0
    )
    table = jnp.asarray(rows.T.astype(np.float32)).astype(jnp.bfloat16)
    vmem = pl.BlockSpec(memory_space=pltpu.VMEM)
    hbm = pl.BlockSpec(memory_space=pl.ANY)
    gathered = pl.pallas_call(
        functools.partial(spectra_kernel, depth, chunks),
        out_shape=pltpu.VMEM((2 * chunks, devices, half, 2 * GROUP, LANES), jnp.bfloat16),
        in_specs=[pl.BlockSpec(memory_space=pltpu.HBM)] * 3,
        out_specs=vmem,
        scratch_shapes=[
            pltpu.VMEM((tap_count, points), jnp.int32),
            pltpu.VMEM((2 * points, 2 * CHANNELS), jnp.bfloat16),
            pltpu.VMEM((2, inputs, samples + (tap_count - 1) * points), jnp.bfloat16),
            pltpu.VMEM((GROUP * inputs, 2 * points), jnp.bfloat16),
            pltpu.VMEM((GROUP * inputs, 2 * CHANNELS), jnp.float32),
            pltpu.VMEM((GROUP * 2 * CHANNELS, inputs), jnp.float32),
            pltpu.VMEM((chunks, CHANNELS, 2 * GROUP, inputs), jnp.bfloat16),
            pltpu.SemaphoreType.DMA((2,)),
            pltpu.SemaphoreType.DMA((chunks,)),
            pltpu.SemaphoreType.DMA((2,)),
            pltpu.SemaphoreType.DMA((chunks,)),
            pltpu.SemaphoreType.DMA((chunks,)),
            pltpu.SemaphoreType.DMA((3, 2 * chunks, depth)),
            pltpu.SemaphoreType.DMA((2 * chunks, devices)),
        ],
        compiler_params=pltpu.CompilerParams(
            collective_id=0, has_side_effects=True, vmem_limit_bytes=40 * 1024 * 1024
        ),
        name="spectra",
    )(*(pltpu.with_memory_space_constraint(a, pltpu.HBM) for a in (filter_taps, table, voltage)))
    buffers = 4
    return pl.pallas_call(
        functools.partial(correlate_kernel, 2 * chunks * GROUP),
        out_shape=jax.ShapeDtypeStruct((2, half, inputs, devices * inputs), jnp.float32),
        in_specs=[vmem],
        out_specs=hbm,
        scratch_shapes=[
            pltpu.VMEM((buffers, 2, inputs, devices * inputs), jnp.float32),
            pltpu.SemaphoreType.DMA((buffers,)),
        ],
        compiler_params=pltpu.CompilerParams(vmem_limit_bytes=20 * 1024 * 1024),
        name="correlate",
    )(gathered)


def body(voltage, filter_taps):
    spectra_here = voltage.shape[2] // filter_taps.shape[1]
    suits = (
        lax.axis_size("slab") == 2
        and lax.axis_size("pol") == 2
        and voltage.shape[1] == LANES
        and filter_taps.shape[1] % 256 == 0
        and spectra_here % GROUP == 0
        and spectra_here >= 2 * GROUP
        and 1 < filter_taps.shape[0] <= GROUP + 1
    )
    return fast_body(voltage, filter_taps) if suits else general_body(voltage, filter_taps)


def solution(mesh):
    placed = (P("band", ("inp", "pol"), "slab"), P())
    return jax.shard_map(
        body,
        mesh=mesh,
        in_specs=placed,
        out_specs=P("band", "slab", ("inp", "pol"), None),
        check_vma=False,
    )
```

```python
import functools
import math

import jax
import jax.numpy as jnp
import numpy as np
from jax import lax
from jax.experimental import pallas as pl
from jax.experimental.pallas import tpu as pltpu
from jax.sharding import PartitionSpec as P

CHANNELS = 64
GROUP = 8
LANES = 128
MESH = pl.DeviceIdType.MESH


def passed_along(value, axis, steps):
    count = lax.axis_size(axis)
    first, last = (max(0, -steps), min(count, count - steps))
    return lax.ppermute(value, axis, [(source, source + steps) for source in range(first, last)])


def dft_table(channel_count, points):
    channel = jnp.arange(channel_count, dtype=jnp.int32)[:, None]
    sample = jnp.arange(points, dtype=jnp.int32)[None, :]
    residue = channel * sample % points
    angles = residue.astype(jnp.float32) * (2.0 * math.pi / points)
    cosine = jnp.cos(angles) / 32.0
    sine_part = jnp.sin(angles) / 32.0
    real_rows = jnp.stack([cosine, sine_part], axis=1)
    imag_rows = jnp.stack([-sine_part, cosine], axis=1)
    return jnp.stack([real_rows, imag_rows], axis=0).astype(jnp.bfloat16)


def filter_bank(voltage, filter_taps, tail_rows):
    tap_count = filter_taps.shape[0]
    points = filter_taps.shape[1]
    extended = jnp.concatenate([tail_rows, voltage], axis=2).astype(jnp.float32)
    spectra_here = voltage.shape[2] // points
    frames = extended.reshape(2, voltage.shape[1], spectra_here + tap_count - 1, points)
    weights = filter_taps.astype(jnp.float32) / 128.0
    filtered = weights[0] * frames[:, :, 0:spectra_here]
    for tap_index in range(1, tap_count):
        filtered = (
            filtered + weights[tap_index] * frames[:, :, tap_index : tap_index + spectra_here]
        )
    return filtered.astype(jnp.bfloat16)


def general_body(voltage, filter_taps):
    points = filter_taps.shape[1]
    tail_length = (filter_taps.shape[0] - 1) * points
    tail_rows = passed_along(voltage[:, :, voltage.shape[2] - tail_length :], "slab", 1)
    filtered = filter_bank(voltage, filter_taps, tail_rows)
    spectra = jnp.einsum(
        "afbp,bisp->fais", dft_table(CHANNELS, points), filtered, preferred_element_type=jnp.float32
    ).astype(jnp.bfloat16)
    turned = lax.all_to_all(spectra, "slab", split_axis=0, concat_axis=3, tiled=True)
    row_count = turned.shape[2]
    left = turned.reshape(turned.shape[0], 2 * row_count, turned.shape[3])
    incoming = lax.all_gather(turned, ("inp", "pol"), axis=2, tiled=True)
    col_count = incoming.shape[2]
    right = incoming.reshape(incoming.shape[0], 2 * col_count, incoming.shape[3])
    products = jnp.einsum("fis,fjs->fij", left, right, preferred_element_type=jnp.float32)
    real_part = products[:, :row_count, :col_count] + products[:, row_count:, col_count:]
    imag_part = products[:, row_count:, :col_count] - products[:, :row_count, col_count:]
    return jnp.stack([real_part, imag_part], axis=0) / (32.0 * turned.shape[3])


def spectra_kernel(
    depth, chunks, taps_hbm, table_hbm, volt_ref, g_ref,
    taps_ref, table_ref, ext, filt, ybuf, tbuf, stage, aux_sem, load_sem, tail_sem, local_sem, x_sem, send_sem, recv_sem,
):
    tap_count, points = taps_ref.shape
    tail = (tap_count - 1) * points
    span = GROUP * points
    half = CHANNELS // 2
    inputs = volt_ref.shape[1]
    z = lax.axis_index("inp")
    x = lax.axis_index("slab")
    c = lax.axis_index("pol")
    me = z * 2 + c
    last = chunks - 1

    barrier = pltpu.get_barrier_semaphore()
    pl.semaphore_signal(barrier, inc=1, device_id={"pol": 1 - c}, device_id_type=MESH)
    pl.semaphore_signal(barrier, inc=1, device_id={"slab": 1 - x}, device_id_type=MESH)

    @pl.when(z > 0)
    def _():
        pl.semaphore_signal(barrier, inc=1, device_id={"inp": z - 1}, device_id_type=MESH)

    @pl.when(z < depth - 1)
    def _():
        pl.semaphore_signal(barrier, inc=1, device_id={"inp": z + 1}, device_id_type=MESH)

    below = jnp.where(z > 0, 1, 0)
    above = jnp.where(z < depth - 1, 1, 0)
    peers = 2 + below + above

    def chunk_of(m):
        return m + x * (last - 2 * m)

    total_span = chunks * span

    def load(n):
        low = n * span + (tail if n else 0)
        size = min(span + (0 if n else tail), total_span - low)
        at = pl.multiple_of(low + x * (total_span - size - 2 * low), points)
        return pltpu.make_async_copy(
            volt_ref.at[:, :, pl.ds(at, size)],
            ext.at[:, :, pl.ds(pl.multiple_of(at + tail, points), size)],
            load_sem.at[n],
        )

    taps_copy = pltpu.make_async_copy(taps_hbm, taps_ref, aux_sem.at[0])
    table_copy = pltpu.make_async_copy(table_hbm, table_ref, aux_sem.at[1])
    def first_load(b):
        size = span + tail
        at = pl.multiple_of(x * (total_span - size), points)
        return pltpu.make_async_copy(
            volt_ref.at[b, :, pl.ds(at, size)],
            ext.at[b, :, pl.ds(pl.multiple_of(at + tail, points), size)],
            aux_sem.at[2 + b],
        )

    first_load(0).start()
    taps_copy.start()
    first_load(1).start()
    table_copy.start()

    @pl.when(x == 0)
    def _():
        ext[:, :, 0:tail] = jnp.zeros((2, inputs, tail), ext.dtype)

    def tail_copy():
        return pltpu.make_async_remote_copy(
            src_ref=volt_ref.at[:, :, pl.ds(chunks * span - tail, tail)],
            dst_ref=ext.at[:, :, pl.ds(0, tail)],
            send_sem=tail_sem.at[0],
            recv_sem=tail_sem.at[1],
            device_id={"slab": 1 - x},
            device_id_type=MESH,
        )

    def compute(m):
        base = pl.multiple_of(chunk_of(m) * span, span)
        wide = 256

        for b in range(2):
            if not isinstance(m, int):

                @pl.when(m == 0)
                def _():
                    first_load(b).wait()
                    if b == 1:
                        for n in range(1, chunks):
                            load(n).start()
                        table_copy.wait()

            for w in range(points // wide):
                scale = [
                    taps_ref[k : k + 1, w * wide : (w + 1) * wide].astype(jnp.float32)
                    * (1.0 / 128.0)
                    for k in range(tap_count)
                ]

                def rows(r, carry):
                    row = pl.multiple_of(r * 16, 16)
                    frames = []
                    for s in range(GROUP + tap_count - 1):
                        at = pl.multiple_of(base + s * points + w * wide, wide)
                        frames.append(
                            ext[b, pl.ds(row, 16), pl.ds(at, wide)].astype(jnp.float32)
                        )
                        if s >= tap_count - 1:
                            first = s - tap_count + 1
                            total = scale[0] * frames[first]
                            for k in range(1, tap_count):
                                total = total + scale[k] * frames[first + k]
                            filt[
                                pl.ds(pl.multiple_of(first * inputs + row, 16), 16),
                                pl.ds(b * points + w * wide, wide),
                            ] = total.astype(jnp.bfloat16)
                    return carry

                lax.fori_loop(0, inputs // 16, rows, 0)
        ybuf[...] = jnp.dot(filt[...], table_ref[...], preferred_element_type=jnp.float32)
        for s in range(GROUP):
            tbuf[s * 2 * CHANNELS : (s + 1) * 2 * CHANNELS, :] = ybuf[
                s * inputs : (s + 1) * inputs, :
            ].T
        for f in range(CHANNELS):
            real = tbuf[pl.ds(f, GROUP, stride=2 * CHANNELS), :]
            imag = tbuf[pl.ds(CHANNELS + f, GROUP, stride=2 * CHANNELS), :]
            stage[m, f] = jnp.concatenate([real, imag], axis=0).astype(jnp.bfloat16)

    def remote(src, q, dev, sem, where):
        return pltpu.make_async_remote_copy(
            src_ref=src,
            dst_ref=g_ref.at[q, dev],
            send_sem=sem,
            recv_sem=recv_sem.at[q, dev],
            device_id=where,
            device_id_type=MESH,
        )

    def up(src, q, zs):
        return remote(src, q, zs * 2 + c, send_sem.at[0, q, zs], {"inp": z + 1})

    def down(src, q, zs):
        return remote(src, q, zs * 2 + c, send_sem.at[1, q, zs], {"inp": z - 1})

    def across(src, q, zs):
        return remote(src, q, zs * 2 + c, send_sem.at[2, q, zs], {"pol": 1 - c})

    def spread(src, q):
        @pl.when(z < depth - 1)
        def _():
            up(src, q, z).start()

        @pl.when(z > 0)
        def _():
            down(src, q, z).start()

        across(src, q, z).start()

    def mine(m):
        return stage.at[m, pl.ds(pl.multiple_of(x * half, half), half)]

    def theirs(m):
        return stage.at[m, pl.ds(pl.multiple_of((1 - x) * half, half), half)]

    def keep(m):
        return pltpu.make_async_copy(mine(m), g_ref.at[x * chunks + m, me], local_sem.at[m])

    def give(m):
        return remote(theirs(m), x * chunks + m, me, x_sem.at[m], {"slab": 1 - x})

    def send_own(m):
        spread(mine(m), x * chunks + m)
        give(m).start()
        keep(m).start()

    def send_given(m):
        q = (1 - x) * chunks + m
        slot = g_ref.at[q, me]
        remote(slot, q, me, x_sem.at[m], {"slab": 1 - x}).wait_recv()
        spread(slot, q)

    def forward(q, distance):
        @pl.when(z - distance >= 0)
        def _():
            zs = z - distance
            slot = g_ref.at[q, zs * 2 + c]
            up(slot, q, zs).wait_recv()

            @pl.when(z < depth - 1)
            def _():
                up(slot, q, zs).start()

            across(slot, q, zs).start()

        @pl.when(z + distance < depth)
        def _():
            zs = z + distance
            slot = g_ref.at[q, zs * 2 + c]
            down(slot, q, zs).wait_recv()

            @pl.when(z > 0)
            def _():
                down(slot, q, zs).start()

            across(slot, q, zs).start()

    taps_copy.wait()

    def early(m, carry):
        compute(m)

        @pl.when(m == 0)
        def _():
            pl.semaphore_wait(barrier, peers)

        send_own(m)
        for n in range(1, chunks):

            @pl.when(m == n - 1)
            def _():
                load(n).wait()

        return carry

    lax.fori_loop(0, last, early, 0)

    @pl.when(x == 0)
    def _():
        tail_copy().start()

    for m in range(last):
        send_given(m)

    def forward_early(distance):
        def step(m, carry):
            forward(m, distance)
            forward(chunks + m, distance)
            return carry

        lax.fori_loop(0, last, step, 0)

    for distance in range(1, depth - 1):
        forward_early(distance)

    @pl.when(x == 1)
    def _():
        tail_copy().wait_recv()

    compute(last)
    send_own(last)
    send_given(last)
    for distance in range(1, depth - 1):
        forward(last, distance)
        forward(chunks + last, distance)
    def finish(q, zs):
        other = zs * 2 + 1 - c
        remote(
            g_ref.at[q, other], q, other, send_sem.at[2, q, zs], {"pol": 1 - c}
        ).wait_recv()
        slot = g_ref.at[q, zs * 2 + c]

        @pl.when((z >= zs) & (z < depth - 1))
        def _():
            up(slot, q, zs).wait_send()

        @pl.when((z <= zs) & (z > 0))
        def _():
            down(slot, q, zs).wait_send()

        across(slot, q, zs).wait_send()

    def far(zs):
        return (z - zs == depth - 1) | (zs - z == depth - 1)

    def finish_near(q, carry):
        for zs in range(depth):

            @pl.when(jnp.logical_not(far(zs)))
            def _():
                finish(q, zs)

        return carry

    def finish_far(q, carry):
        for zs in (0, depth - 1):

            @pl.when(far(zs))
            def _():
                finish(q, zs)

        return carry

    lax.fori_loop(0, 2 * chunks, finish_near, 0)
    for m in range(chunks):
        keep(m).wait()
        give(m).wait_send()

    @pl.when(x == 0)
    def _():
        tail_copy().wait_send()

    forward_early(depth - 1)
    forward(last, depth - 1)
    forward(chunks + last, depth - 1)
    lax.fori_loop(0, 2 * chunks, finish_far, 0)


def correlate_kernel(spectra_total, g_ref, out_ref, buf, sem):
    slots, devices, channels, rows, lanes = g_ref.shape
    depth = buf.shape[0]
    me = lax.axis_index("inp") * 2 + lax.axis_index("pol")
    scale = 1.0 / (32.0 * spectra_total)

    def put(f, slot):
        return pltpu.make_async_copy(buf.at[slot], out_ref.at[:, f], sem.at[slot])

    def step(f, carry):
        slot = lax.rem(f, depth)

        @pl.when(f >= depth)
        def _():
            put(f - depth, slot).wait()

        own = g_ref[:, me, f].astype(jnp.float32) * scale
        real, imag = own[:, : rows // 2], own[:, rows // 2 :]
        straight = own.reshape(slots * rows, lanes).T
        crossed = jnp.concatenate([imag, -real], axis=1).reshape(slots * rows, lanes).T
        left = jnp.concatenate([straight, crossed], axis=0).astype(jnp.bfloat16)
        right = jnp.concatenate(
            [g_ref[:, j, f].reshape(slots * rows, lanes) for j in range(devices)], axis=1
        )
        product = jnp.dot(left, right, preferred_element_type=jnp.float32)
        buf[slot, 0] = product[:lanes]
        buf[slot, 1] = product[lanes:]
        put(f, slot).start()
        return carry

    lax.fori_loop(0, channels, step, 0)
    for f in range(channels - depth, channels):
        put(f, f % depth).wait()


def fast_body(voltage, filter_taps):
    depth = lax.axis_size("inp")
    tap_count, points = filter_taps.shape
    inputs, samples = voltage.shape[1:]
    chunks = samples // points // GROUP
    half = CHANNELS // 2
    devices = depth * 2
    channel = np.arange(CHANNELS, dtype=np.int64)[:, None]
    angles = (channel * np.arange(points)[None, :] % points).astype(np.float32)
    angles = (angles * np.float32(2.0 * math.pi / points)).astype(np.float64)
    cosine, sine = np.cos(angles) / 32.0, np.sin(angles) / 32.0
    rows = np.concatenate(
        [np.concatenate([cosine, sine], 1), np.concatenate([-sine, cosine], 1)], 0
    )
    table = jnp.asarray(rows.T.astype(np.float32)).astype(jnp.bfloat16)
    vmem = pl.BlockSpec(memory_space=pltpu.VMEM)
    hbm = pl.BlockSpec(memory_space=pl.ANY)
    gathered = pl.pallas_call(
        functools.partial(spectra_kernel, depth, chunks),
        out_shape=pltpu.VMEM((2 * chunks, devices, half, 2 * GROUP, LANES), jnp.bfloat16),
        in_specs=[pl.BlockSpec(memory_space=pltpu.HBM)] * 3,
        out_specs=vmem,
        scratch_shapes=[
            pltpu.VMEM((tap_count, points), jnp.int32),
            pltpu.VMEM((2 * points, 2 * CHANNELS), jnp.bfloat16),
            pltpu.VMEM((2, inputs, samples + (tap_count - 1) * points), jnp.bfloat16),
            pltpu.VMEM((GROUP * inputs, 2 * points), jnp.bfloat16),
            pltpu.VMEM((GROUP * inputs, 2 * CHANNELS), jnp.float32),
            pltpu.VMEM((GROUP * 2 * CHANNELS, inputs), jnp.float32),
            pltpu.VMEM((chunks, CHANNELS, 2 * GROUP, inputs), jnp.bfloat16),
            pltpu.SemaphoreType.DMA((4,)),
            pltpu.SemaphoreType.DMA((chunks,)),
            pltpu.SemaphoreType.DMA((2,)),
            pltpu.SemaphoreType.DMA((chunks,)),
            pltpu.SemaphoreType.DMA((chunks,)),
            pltpu.SemaphoreType.DMA((3, 2 * chunks, depth)),
            pltpu.SemaphoreType.DMA((2 * chunks, devices)),
        ],
        compiler_params=pltpu.CompilerParams(
            collective_id=0, has_side_effects=True, vmem_limit_bytes=40 * 1024 * 1024
        ),
        name="spectra",
    )(*(pltpu.with_memory_space_constraint(a, pltpu.HBM) for a in (filter_taps, table, voltage)))
    buffers = 4
    return pl.pallas_call(
        functools.partial(correlate_kernel, 2 * chunks * GROUP),
        out_shape=jax.ShapeDtypeStruct((2, half, inputs, devices * inputs), jnp.float32),
        in_specs=[vmem],
        out_specs=hbm,
        scratch_shapes=[
            pltpu.VMEM((buffers, 2, inputs, devices * inputs), jnp.float32),
            pltpu.SemaphoreType.DMA((buffers,)),
        ],
        compiler_params=pltpu.CompilerParams(vmem_limit_bytes=20 * 1024 * 1024),
        name="correlate",
    )(gathered)


def body(voltage, filter_taps):
    spectra_here = voltage.shape[2] // filter_taps.shape[1]
    suits = (
        lax.axis_size("slab") == 2
        and lax.axis_size("pol") == 2
        and voltage.shape[1] == LANES
        and filter_taps.shape[1] % 256 == 0
        and spectra_here % GROUP == 0
        and spectra_here >= 2 * GROUP
        and 1 < filter_taps.shape[0] <= GROUP + 1
    )
    return fast_body(voltage, filter_taps) if suits else general_body(voltage, filter_taps)


def solution(mesh):
    placed = (P("band", ("inp", "pol"), "slab"), P())
    return jax.shard_map(
        body,
        mesh=mesh,
        in_specs=placed,
        out_specs=P("band", "slab", ("inp", "pol"), None),
        check_vma=False,
    )
```
